256 devices in a mesh: lat: 8 (over x, y_lo), lon: 32 (over y_hi, z, core).
Axes of the slice: x: 4, y: 4 (y_hi: 2, y_lo: 2; y = y_hi * 2 + y_lo), z: 8, core: 2. Of those that a mesh axis runs over, the one named last changes fastest.
Arguments:
- tracers: float32 [2, 12, 128, 4096], P(None, None, 'lat', 'lon'), may hold values from -6 to 6
- wet_levels: int32 [128, 4096], P('lat', 'lon'), may hold values from 0 to 12, as said below
- east_speed: float32 [12, 128, 4096], P(None, 'lat', 'lon'), may hold values from -0.25 to 0.25
- north_speed: float32 [12, 128, 4096], P(None, 'lat', 'lon'), may hold values from -0.25 to 0.25
- down_speed: float32 [12, 128, 4096], P(None, 'lat', 'lon'), may hold values from -0.25 to 0.25
- east_diffusivity: float32 [12, 128, 4096], P(None, 'lat', 'lon'), may hold values from 0.02 to 0.12
- east_slope: float32 [12, 128, 4096], P(None, 'lat', 'lon'), may hold values from -1 to 1
- north_diffusivity: float32 [12, 128, 4096], P(None, 'lat', 'lon'), may hold values from 0.02 to 0.12
- north_slope: float32 [12, 128, 4096], P(None, 'lat', 'lon'), may hold values from -1 to 1
- down_diffusivity: float32 [12, 128, 4096], P(None, 'lat', 'lon'), may hold values from 0.02 to 0.12
- down_slope_east: float32 [12, 128, 4096], P(None, 'lat', 'lon'), may hold values from -1 to 1
- down_slope_north: float32 [12, 128, 4096], P(None, 'lat', 'lon'), may hold values from -1 to 1
Outputs:
- evolved_tracers: float32 [2, 12, 128, 4096], P(None, None, 'lat', 'lon')
The draws below stay inside these ranges and needn't reach their ends.
Inputs may be any that keep to these rules, and one draw needn't show every extreme that they name: `wet_levels`: 0 marks a land column. Land comes as single columns, as aligned blocks of 8 x 8 columns and as whole aligned blocks of 16 x 128 columns.
All inputs are finite; a program needn't handle non-finite values.
Results may differ from the reference program's by a relative error of at most 0.0003.
Values sent between devices are 32-bit elements; how exact they have to be, the bound alone decides.
No kernel may reach another device: no remote copies, remote signals or barrier semaphores. Data moves between devices by JAX's collectives and lax.ppermute only.
A program may use at most 64 MiB of HBM per device.

```python
import math
import jax
import jax.numpy as jnp
from jax import lax

NTR = 2
K = 12
CJ = 16
CI = 128
STEPS = 3
NJ = 128
NI = 4096


def draw_wet_levels(key, part):
    key = jax.random.fold_in(key, 7)
    depth_key, cell_key, patch_key, block_key = jax.random.split(key, 4)
    column_depth = jax.random.randint(depth_key, (NJ, NI), 1, K + 1)
    cell_land = jax.random.randint(cell_key, (NJ, NI), 0, 8) == 0
    patch_flags = jax.random.randint(patch_key, (NJ // 8, NI // 8), 0, 4) == 0
    patch_land = jnp.repeat(jnp.repeat(patch_flags, 8, axis=0), 8, axis=1)
    block_flags = jax.random.randint(block_key, (NJ // CJ, NI // CI), 0, 6) == 0
    block_land = jnp.repeat(jnp.repeat(block_flags, CJ, axis=0), CI, axis=1)
    return jnp.where(cell_land | patch_land | block_land, 0, column_depth).astype(jnp.int32)


def block_scale(key, dims, shards, least, high):
    level = 1.0
    for position, parts in shards:
        heights = jax.random.uniform(jax.random.fold_in(jax.random.fold_in(key, 6), position), (parts,), jnp.float32, least / len(shards), high / len(shards))
        level = level * jnp.repeat(jnp.exp(heights), dims[position] // parts).reshape((-1,) + (1,) * (len(dims) - 1 - position))
    return level


def gaussian(rng, dims, deviation, most, cuts=(), kind=jnp.bfloat16):
    array = deviation * jax.random.normal(rng, dims, jnp.float32)
    if cuts:
        array = array * block_scale(rng, dims, cuts, -0.22, 0.18)
    return jnp.clip(array, -most, most).astype(kind)


def setup_inputs(seed: int = 0) -> dict:
    seeds = jax.random.split(jax.random.key(seed), 13)
    tracers = gaussian(seeds[0], (NTR, K, NJ, NI), 1.0, 6.0, ((2, 8), (3, 32)), jnp.float32)
    wet_levels = draw_wet_levels(jax.random.fold_in(seeds[12], 71), 0)
    east_speed = gaussian(seeds[2], (K, NJ, NI), 0.1, 0.25, ((1, 8), (2, 32)), jnp.float32)
    north_speed = gaussian(seeds[3], (K, NJ, NI), 0.1, 0.25, ((1, 8), (2, 32)), jnp.float32)
    down_speed = gaussian(seeds[4], (K, NJ, NI), 0.1, 0.25, ((1, 8), (2, 32)), jnp.float32)
    east_diffusivity = jnp.clip(jnp.exp(math.log(0.12) - 1.7917595 * jax.random.uniform(seeds[5], (K, NJ, NI), jnp.float32) ** block_scale(seeds[5], (K, NJ, NI), ((1, 8), (2, 32)), -0.2, 0.2)), 0.02, 0.12)
    east_slope = gaussian(seeds[6], (K, NJ, NI), 0.4, 1.0, ((1, 8), (2, 32)), jnp.float32)
    north_diffusivity = jnp.clip(jnp.exp(math.log(0.12) - 1.7917595 * jax.random.uniform(seeds[7], (K, NJ, NI), jnp.float32) ** block_scale(seeds[7], (K, NJ, NI), ((1, 8), (2, 32)), -0.2, 0.2)), 0.02, 0.12)
    north_slope = gaussian(seeds[8], (K, NJ, NI), 0.4, 1.0, ((1, 8), (2, 32)), jnp.float32)
    down_diffusivity = jnp.clip(jnp.exp(math.log(0.12) - 1.7917595 * jax.random.uniform(seeds[9], (K, NJ, NI), jnp.float32) ** block_scale(seeds[9], (K, NJ, NI), ((1, 8), (2, 32)), -0.2, 0.2)), 0.02, 0.12)
    down_slope_east = gaussian(seeds[10], (K, NJ, NI), 0.4, 1.0, ((1, 8), (2, 32)), jnp.float32)
    down_slope_north = gaussian(seeds[11], (K, NJ, NI), 0.4, 1.0, ((1, 8), (2, 32)), jnp.float32)
    return {"tracers": tracers, "wet_levels": wet_levels, "east_speed": east_speed, "north_speed": north_speed, "down_speed": down_speed, "east_diffusivity": east_diffusivity, "east_slope": east_slope, "north_diffusivity": north_diffusivity, "north_slope": north_slope, "down_diffusivity": down_diffusivity, "down_slope_east": down_slope_east, "down_slope_north": down_slope_north}


def take_span(values, first_index, last_index, along_axis):
    return lax.slice_in_dim(values, first_index, last_index, axis=along_axis)


def minmod(left_jump, right_jump):
    return 0.5 * (jnp.sign(left_jump) + jnp.sign(right_jump)) * jnp.minimum(jnp.abs(left_jump), jnp.abs(right_jump))


def advect(values, flow_speed, face_mask, along_axis):
    length = values.shape[along_axis]
    jumps = (take_span(values, 1, length, along_axis) - take_span(values, 0, length - 1, along_axis)) * face_mask
    slopes = minmod(take_span(jumps, 0, length - 2, along_axis), take_span(jumps, 1, length - 1, along_axis))
    velocity = take_span(flow_speed, 1, length - 2, along_axis)
    courant = 1.0 - jnp.abs(velocity)
    from_below = take_span(values, 1, length - 2, along_axis) + 0.5 * courant * take_span(slopes, 0, length - 3, along_axis)
    from_above = take_span(values, 2, length - 1, along_axis) - 0.5 * courant * take_span(slopes, 1, length - 2, along_axis)
    return velocity * jnp.where(velocity > 0, from_below, from_above) * take_span(face_mask, 1, length - 2, along_axis)


def tendency(ext_tracer, wet_ext, east_ext, north_ext, diff_east_ext, slope_east_ext, diff_north_ext, slope_north_ext, down_speed, down_diffusivity, down_slope_east, down_slope_north):
    levels_count, rows_ext, cols_ext = ext_tracer.shape
    inner = (slice(None), slice(2, rows_ext - 2), slice(2, cols_ext - 2))
    mask_east = take_span(wet_ext, 0, cols_ext - 1, 2) * take_span(wet_ext, 1, cols_ext, 2)
    mask_north = take_span(wet_ext, 0, rows_ext - 1, 1) * take_span(wet_ext, 1, rows_ext, 1)
    flux_east = advect(ext_tracer, east_ext, mask_east, 2)
    flux_north = advect(ext_tracer, north_ext, mask_north, 1)
    transport = (take_span(flux_east, 1, cols_ext - 3, 2) - take_span(flux_east, 0, cols_ext - 4, 2))[:, 2:rows_ext - 2, :]
    transport = transport + (take_span(flux_north, 1, rows_ext - 3, 1) - take_span(flux_north, 0, rows_ext - 4, 1))[:, :, 2:cols_ext - 2]
    centre = ext_tracer[inner]
    wet_centre = wet_ext[inner]
    pad_spec = ((2, 2), (0, 0), (0, 0))
    padded_wet = jnp.pad(wet_centre, pad_spec)
    flux_below = advect(jnp.pad(centre, pad_spec), jnp.pad(down_speed, pad_spec), padded_wet[:-1] * padded_wet[1:], 0)
    transport = transport + (flux_below[1:levels_count + 1] - flux_below[:levels_count])
    mask_below = wet_ext[1:] * wet_ext[:-1]
    jump_below = (ext_tracer[1:] - ext_tracer[:-1]) * mask_below
    zero_layer = jnp.zeros_like(ext_tracer[:1])
    jump_padded = jnp.concatenate([zero_layer, jump_below, zero_layer], axis=0)
    vertical_grad = 0.5 * (jump_padded[:-1] + jump_padded[1:])
    grad_east = (take_span(ext_tracer, 1, cols_ext, 2) - take_span(ext_tracer, 0, cols_ext - 1, 2)) * mask_east
    grad_north = (take_span(ext_tracer, 1, rows_ext, 1) - take_span(ext_tracer, 0, rows_ext - 1, 1)) * mask_north
    tilt_east = 0.5 * (take_span(vertical_grad, 0, cols_ext - 1, 2) + take_span(vertical_grad, 1, cols_ext, 2)) * mask_east
    tilt_north = 0.5 * (take_span(vertical_grad, 0, rows_ext - 1, 1) + take_span(vertical_grad, 1, rows_ext, 1)) * mask_north
    spread_east = take_span(diff_east_ext, 0, cols_ext - 1, 2) * (grad_east + take_span(slope_east_ext, 0, cols_ext - 1, 2) * tilt_east)
    spread_north = take_span(diff_north_ext, 0, rows_ext - 1, 1) * (grad_north + take_span(slope_north_ext, 0, rows_ext - 1, 1) * tilt_north)
    mixing = (take_span(spread_east, 2, cols_ext - 2, 2) - take_span(spread_east, 1, cols_ext - 3, 2))[:, 2:rows_ext - 2, :]
    mixing = mixing + (take_span(spread_north, 2, rows_ext - 2, 1) - take_span(spread_north, 1, rows_ext - 3, 1))[:, :, 2:cols_ext - 2]
    east_centre = (0.5 * (take_span(grad_east, 1, cols_ext - 3, 2) + take_span(grad_east, 2, cols_ext - 2, 2)))[:, 2:rows_ext - 2, :]
    north_centre = (0.5 * (take_span(grad_north, 1, rows_ext - 3, 1) + take_span(grad_north, 2, rows_ext - 2, 1)))[:, :, 2:cols_ext - 2]
    slope_along = down_slope_east[:-1]
    slope_across = down_slope_north[:-1]
    vertical_flux = down_diffusivity[:-1] * (slope_along * 0.5 * (east_centre[:-1] + east_centre[1:]) + slope_across * 0.5 * (north_centre[:-1] + north_centre[1:]) + (slope_along * slope_along + slope_across * slope_across) * jump_below[inner]) * mask_below[inner]
    zero_inner = jnp.zeros_like(centre[:1])
    vertical_padded = jnp.concatenate([zero_inner, vertical_flux, zero_inner], axis=0)
    mixing = mixing + (vertical_padded[1:] - vertical_padded[:-1])
    return wet_centre * (mixing - transport)


def extend_global(stacked):
    wrapped = jnp.concatenate([stacked[..., -2:], stacked, stacked[..., :2]], axis=-1)
    folded = jnp.flip(wrapped[..., -2:, :], axis=(-2, -1))
    southern = jnp.zeros_like(wrapped[..., :2, :])
    return jnp.concatenate([southern, wrapped, folded], axis=-2)


def reference(tracers, wet_levels, east_speed, north_speed, down_speed, east_diffusivity, east_slope, north_diffusivity, north_slope, down_diffusivity, down_slope_east, down_slope_north):
    levels = jnp.arange(tracers.shape[1], dtype=jnp.int32)
    wet = (levels[:, None, None] < wet_levels[None]).astype(jnp.float32)
    statics = extend_global(jnp.stack([wet, east_speed, north_speed, east_diffusivity, east_slope, north_diffusivity, north_slope]))
    for step_index in range(STEPS):
        ext_tracers = extend_global(tracers)
        change = jnp.stack([tendency(ext_tracers[tracer_slot], statics[0], statics[1], statics[2], statics[3], statics[4], statics[5], statics[6], down_speed, down_diffusivity, down_slope_east, down_slope_north) for tracer_slot in range(tracers.shape[0])])
        tracers = tracers + change
    return tracers
```

```python
import jax
import jax.numpy as jnp
from jax import lax
from jax.sharding import PartitionSpec as P

STEPS = 3


def swaps(count, first, wrap):
    pairs = []
    for low in range(first, count if wrap else count - 1, 2):
        high = (low + 1) % count
        pairs += [(low, high), (high, low)]
    return pairs


def exchange_lon(to_east, to_west):
    count = lax.axis_size("lon")
    even = lax.axis_index("lon") % 2 == 0
    near = lax.ppermute(jnp.where(even, to_east, to_west), "lon", swaps(count, 0, False))
    far = lax.ppermute(jnp.where(even, to_west, to_east), "lon", swaps(count, 1, True))
    return jnp.where(even, far, near), jnp.where(even, near, far)


def exchange_lat(to_north, to_south):
    bands, count = lax.axis_size("lat"), lax.axis_size("lon")
    even = lax.axis_index("lat") % 2 == 0
    top = lax.axis_index("lat") == bands - 1
    near = lax.ppermute(jnp.where(even, to_north, to_south), "lat", swaps(bands, 0, False))
    pairs = [
        (low * count + i, high * count + i)
        for low, high in swaps(bands, 1, False)
        for i in range(count)
    ]
    pairs += [
        ((bands - 1) * count + i, (bands - 1) * count + count - 1 - i) for i in range(count)
    ]
    far = lax.ppermute(jnp.where(even, to_south, to_north), ("lat", "lon"), pairs)
    from_north = jnp.where(even, near, jnp.where(top, jnp.flip(far, axis=(-2, -1)), far))
    return jnp.where(even, far, near), from_north


def take_span(values, first_index, last_index, along_axis):
    return lax.slice_in_dim(values, first_index, last_index, axis=along_axis)


def minmod(left_jump, right_jump):
    return (
        0.5
        * (jnp.sign(left_jump) + jnp.sign(right_jump))
        * jnp.minimum(jnp.abs(left_jump), jnp.abs(right_jump))
    )


def advect(values, flow_speed, face_mask, along_axis):
    length = values.shape[along_axis]
    jumps = (
        take_span(values, 1, length, along_axis) - take_span(values, 0, length - 1, along_axis)
    ) * face_mask
    slopes = minmod(
        take_span(jumps, 0, length - 2, along_axis), take_span(jumps, 1, length - 1, along_axis)
    )
    velocity = take_span(flow_speed, 1, length - 2, along_axis)
    courant = 1.0 - jnp.abs(velocity)
    from_below = take_span(values, 1, length - 2, along_axis) + 0.5 * courant * take_span(
        slopes, 0, length - 3, along_axis
    )
    from_above = take_span(values, 2, length - 1, along_axis) - 0.5 * courant * take_span(
        slopes, 1, length - 2, along_axis
    )
    return (
        velocity
        * jnp.where(velocity > 0, from_below, from_above)
        * take_span(face_mask, 1, length - 2, along_axis)
    )


def tendency(
    ext_tracer,
    wet_ext,
    east_ext,
    north_ext,
    diff_east_ext,
    slope_east_ext,
    diff_north_ext,
    slope_north_ext,
    down_speed,
    down_diffusivity,
    down_slope_east,
    down_slope_north,
):
    levels_count, rows_ext, cols_ext = ext_tracer.shape
    inner = (slice(None), slice(2, rows_ext - 2), slice(2, cols_ext - 2))
    mask_east = take_span(wet_ext, 0, cols_ext - 1, 2) * take_span(wet_ext, 1, cols_ext, 2)
    mask_north = take_span(wet_ext, 0, rows_ext - 1, 1) * take_span(wet_ext, 1, rows_ext, 1)
    flux_east = advect(ext_tracer, east_ext, mask_east, 2)
    flux_north = advect(ext_tracer, north_ext, mask_north, 1)
    transport = (
        take_span(flux_east, 1, cols_ext - 3, 2) - take_span(flux_east, 0, cols_ext - 4, 2)
    )[:, 2 : rows_ext - 2, :]
    transport = (
        transport
        + (take_span(flux_north, 1, rows_ext - 3, 1) - take_span(flux_north, 0, rows_ext - 4, 1))[
            :, :, 2 : cols_ext - 2
        ]
    )
    centre = ext_tracer[inner]
    wet_centre = wet_ext[inner]
    pad_spec = ((2, 2), (0, 0), (0, 0))
    padded_wet = jnp.pad(wet_centre, pad_spec)
    flux_below = advect(
        jnp.pad(centre, pad_spec),
        jnp.pad(down_speed, pad_spec),
        padded_wet[:-1] * padded_wet[1:],
        0,
    )
    transport = transport + (flux_below[1 : levels_count + 1] - flux_below[:levels_count])
    mask_below = wet_ext[1:] * wet_ext[:-1]
    jump_below = (ext_tracer[1:] - ext_tracer[:-1]) * mask_below
    zero_layer = jnp.zeros_like(ext_tracer[:1])
    jump_padded = jnp.concatenate([zero_layer, jump_below, zero_layer], axis=0)
    vertical_grad = 0.5 * (jump_padded[:-1] + jump_padded[1:])
    grad_east = (
        take_span(ext_tracer, 1, cols_ext, 2) - take_span(ext_tracer, 0, cols_ext - 1, 2)
    ) * mask_east
    grad_north = (
        take_span(ext_tracer, 1, rows_ext, 1) - take_span(ext_tracer, 0, rows_ext - 1, 1)
    ) * mask_north
    tilt_east = (
        0.5
        * (take_span(vertical_grad, 0, cols_ext - 1, 2) + take_span(vertical_grad, 1, cols_ext, 2))
        * mask_east
    )
    tilt_north = (
        0.5
        * (take_span(vertical_grad, 0, rows_ext - 1, 1) + take_span(vertical_grad, 1, rows_ext, 1))
        * mask_north
    )
    spread_east = take_span(diff_east_ext, 0, cols_ext - 1, 2) * (
        grad_east + take_span(slope_east_ext, 0, cols_ext - 1, 2) * tilt_east
    )
    spread_north = take_span(diff_north_ext, 0, rows_ext - 1, 1) * (
        grad_north + take_span(slope_north_ext, 0, rows_ext - 1, 1) * tilt_north
    )
    mixing = (
        take_span(spread_east, 2, cols_ext - 2, 2) - take_span(spread_east, 1, cols_ext - 3, 2)
    )[:, 2 : rows_ext - 2, :]
    mixing = (
        mixing
        + (
            take_span(spread_north, 2, rows_ext - 2, 1)
            - take_span(spread_north, 1, rows_ext - 3, 1)
        )[:, :, 2 : cols_ext - 2]
    )
    east_centre = (
        0.5 * (take_span(grad_east, 1, cols_ext - 3, 2) + take_span(grad_east, 2, cols_ext - 2, 2))
    )[:, 2 : rows_ext - 2, :]
    north_centre = (
        0.5
        * (take_span(grad_north, 1, rows_ext - 3, 1) + take_span(grad_north, 2, rows_ext - 2, 1))
    )[:, :, 2 : cols_ext - 2]
    slope_along = down_slope_east[:-1]
    slope_across = down_slope_north[:-1]
    vertical_flux = (
        down_diffusivity[:-1]
        * (
            slope_along * 0.5 * (east_centre[:-1] + east_centre[1:])
            + slope_across * 0.5 * (north_centre[:-1] + north_centre[1:])
            + (slope_along * slope_along + slope_across * slope_across) * jump_below[inner]
        )
        * mask_below[inner]
    )
    zero_inner = jnp.zeros_like(centre[:1])
    vertical_padded = jnp.concatenate([zero_inner, vertical_flux, zero_inner], axis=0)
    mixing = mixing + (vertical_padded[1:] - vertical_padded[:-1])
    return wet_centre * (mixing - transport)


def extend(stacked, width):
    west, east = exchange_lon(stacked[..., -width:], stacked[..., :width])
    south, north = exchange_lat(stacked[..., -width:, :], stacked[..., :width, :])
    side = ((0, 0),) * (stacked.ndim - 1) + ((width, width),)
    middle = jnp.concatenate([west, stacked, east], axis=-1)
    return jnp.concatenate([jnp.pad(south, side), middle, jnp.pad(north, side)], axis=-2)


def all_tendencies(ext_tracers, fields, downs):
    return jnp.stack(
        [
            tendency(
                ext_tracers[tracer_slot],
                fields[0],
                fields[1],
                fields[2],
                fields[3],
                fields[4],
                fields[5],
                fields[6],
                downs[0],
                downs[1],
                downs[2],
                downs[3],
            )
            for tracer_slot in range(ext_tracers.shape[0])
        ]
    )


def body(
    tracers,
    wet_levels,
    east_speed,
    north_speed,
    down_speed,
    east_diffusivity,
    east_slope,
    north_diffusivity,
    north_slope,
    down_diffusivity,
    down_slope_east,
    down_slope_north,
):
    levels = jnp.arange(tracers.shape[1], dtype=jnp.int32)
    wet = (levels[:, None, None] < wet_levels[None]).astype(jnp.float32)
    statics = extend(
        jnp.stack(
            [
                wet,
                east_speed,
                north_speed,
                east_diffusivity,
                east_slope,
                north_diffusivity,
                north_slope,
            ]
        ),
        2,
    )
    downs = (down_speed, down_diffusivity, down_slope_east, down_slope_north)
    for step_index in range(STEPS):
        ext_tracers = extend(tracers, 2)
        tracers = tracers + all_tendencies(ext_tracers, statics, downs)
    return tracers


def solution(mesh):
    in_specs = (
        P(None, None, "lat", "lon"),
        P("lat", "lon"),
        P(None, "lat", "lon"),
        P(None, "lat", "lon"),
        P(None, "lat", "lon"),
        P(None, "lat", "lon"),
        P(None, "lat", "lon"),
        P(None, "lat", "lon"),
        P(None, "lat", "lon"),
        P(None, "lat", "lon"),
        P(None, "lat", "lon"),
        P(None, "lat", "lon"),
    )
    out_specs = P(None, None, "lat", "lon")
    return jax.shard_map(body, mesh=mesh, in_specs=in_specs, out_specs=out_specs, check_vma=False)
```

```python
import jax
import jax.numpy as jnp
from jax import lax
from jax.experimental import pallas as pl
from jax.experimental.pallas import tpu as pltpu
from jax.sharding import PartitionSpec as P

STEPS = 3
K = 12
ROWS = 16
LANES = 128
EXT = 32
PAD = 48
NORTHWARD = (3, 4, 5)
EASTWARD = (0, 1, 2)
FLIPPED = (0, 2, 3, 5, 8, 9)
STATICS = 10
SLOTS = 19
VMEM_LIMIT = 48 * 1024 * 1024
FULL = 63 * 1024 * 1024


def lane_roll(x, shift):
    return pltpu.roll(x, shift % x.shape[-1], x.ndim - 1)


def row_roll(x, shift):
    return pltpu.roll(x, shift % x.shape[0], 0)


def lanes_of(shape):
    return lax.broadcasted_iota(jnp.int32, shape, len(shape) - 1)


def is_even(axis):
    return lax.rem(lax.axis_index(axis), 2) == 0


def is_top():
    return lax.axis_index("lat") == lax.axis_size("lat") - 1


def pack_band(dst, tracers, levels, statics, northward):
    low4 = ROWS - 4 if northward else 0
    low6 = ROWS - 6 if northward else 0
    extra = ROWS - 5 if northward else 0
    for k in range(K):
        for f in range(STATICS):
            dst[k, 4 * f : 4 * f + 4, :] = statics[f][k, low4 : low4 + 4, :]
        for t in range(2):
            dst[k, 40 + 6 * t : 46 + 6 * t, :] = tracers[t, k, low6 : low6 + 6, :]
        for n, f in enumerate(NORTHWARD):
            dst[k, 52 + n : 53 + n, :] = statics[f][k, extra : extra + 1, :]
        row = low6 + k if k < 6 else 0
        dst[k, 55:56, :] = levels[row : row + 1, :].astype(jnp.float32)


def band_kernel(tracers, levels, *refs):
    statics, (_, near, far) = refs[:STATICS], refs[STATICS:]
    even = is_even("lat")

    @pl.when(even)
    def _():
        pack_band(near, tracers, levels, statics, True)
        pack_band(far, tracers, levels, statics, False)

    @pl.when(jnp.logical_not(even))
    def _():
        pack_band(far, tracers, levels, statics, True)
        pack_band(near, tracers, levels, statics, False)


def side_kernel(tracers, levels, *refs):
    statics, (sides,) = refs[:STATICS], refs[STATICS:]
    place = lanes_of((8, LANES)) // 16
    for tile in range(2):
        rows = slice(8 * tile, 8 * tile + 8)
        for v in range(SLOTS):
            packed = jnp.zeros((8, LANES), jnp.float32)
            for q in range(8):
                slot = 8 * v + q
                f, k = slot // K, slot % K
                if slot == 12 * K:
                    value = levels[rows, :].astype(jnp.float32)
                elif slot > 12 * K:
                    continue
                elif f < STATICS:
                    value = statics[f][k, rows, :]
                else:
                    value = tracers[f - STATICS, k, rows, :]
                packed = jnp.where(place == q, lane_roll(value, 8 + 16 * q), packed)
            sides[tile, v] = packed


def corner_kernel(near_side, far_side, merged, near, far):
    even_lon, even_lat = is_even("lon"), is_even("lat")
    low = lanes_of((8, LANES)) % 16 < 8
    for tile in range(2):
        for v in range(SLOTS):
            a, b = near_side[tile, v], far_side[tile, v]
            east = jnp.where(even_lon, a, b)
            west = jnp.where(even_lon, b, a)
            merged[tile, v] = jnp.where(low, lane_roll(east, -8), lane_roll(west, 8))
    for v in range(SLOTS):
        bottom, top = merged[0, v], merged[1, v]
        near[v] = jnp.where(even_lat, top, bottom)
        far[v] = jnp.where(even_lat, bottom, top)


def minmod(p, q):
    return jnp.maximum(jnp.minimum(p, q), 0.0) + jnp.minimum(jnp.maximum(p, q), 0.0)


def signed_half(c):
    return jnp.where(c > 0, 0.5, -0.5) - 0.5 * c


def face_flux(c, h, spread, tilt, here, there, before, jump, after, grads):
    up = c > 0
    slope = minmod(jnp.where(up, before, after), jump)
    return c * (jnp.where(up, here, there) + h * slope) - spread * (jump + tilt * grads)


def at(tile, shift=0):
    return slice(8 + 8 * tile + shift, 16 + 8 * tile + shift)


def plain(tile):
    return slice(8 * tile, 8 * tile + 8)


def level_tables(level, table):
    table[0, 8 : 8 + EXT, :] = level
    table[1, 8 : 8 + EXT, :] = jnp.minimum(level, lane_roll(level, -1))
    table[2, 8 : 8 + EXT, :] = jnp.minimum(level, row_roll(level, -1))


def derive(raw, put, seam_raw, seam_put, table):
    for tile in range(4):
        rows = plain(tile)
        level, east_level, north_level = (table[i, at(tile), :] for i in range(3))
        for k in range(K):
            east, north, lower = east_level > k, north_level > k, level > k + 1
            c = raw[0, k, rows, :]
            put[0, k, rows, :] = jnp.where(east, c, 0.0)
            put[1, k, rows, :] = signed_half(c)
            put[2, k, rows, :] = raw[1, k, rows, :]
            put[3, k, rows, :] = jnp.where(east, 0.25 * raw[2, k, rows, :], 0.0)
            c = raw[3, k, rows, :]
            put[4, k, rows, :] = jnp.where(north, c, 0.0)
            put[5, k, rows, :] = signed_half(c)
            put[6, k, rows, :] = raw[4, k, rows, :]
            put[7, k, rows, :] = jnp.where(north, 0.25 * raw[5, k, rows, :], 0.0)
            if tile == 2:
                c = seam_raw[0, k]
                seam_put[0, k] = jnp.where(north, c, 0.0)
                seam_put[1, k] = signed_half(c)
                seam_put[2, k] = seam_raw[1, k]
                seam_put[3, k] = jnp.where(north, 0.25 * seam_raw[2, k], 0.0)
            if k < K - 1:
                c, spread = raw[6, k, rows, :], raw[7, k, rows, :]
                along, across = raw[8, k, rows, :], raw[9, k, rows, :]
                put[8, k, rows, :] = jnp.where(lower, c, 0.0)
                put[9, k, rows, :] = signed_half(c)
                put[10, k, rows, :] = spread * (along * along + across * across)
                masked = jnp.where(lower, 0.25 * spread, 0.0)
                put[11, k, rows, :] = masked * along
                put[12, k, rows, :] = masked * across


def grads_pass(x, doms, table, dz, tz):
    for tile in range(4):
        level = table[0, at(tile), :]
        for dom in doms:
            above = None
            here = x[dom, 0, at(tile), :]
            for k in range(K):
                if k < K - 1:
                    below = x[dom, k + 1, at(tile), :]
                    d = jnp.where(level > k + 1, below - here, 0.0)
                    dz[dom, k, plain(tile), :] = d
                    tz[dom, k, at(tile), :] = d if above is None else above + d
                    here, above = below, d
                else:
                    tz[dom, k, at(tile), :] = above


def sides_pass(x, doms, table, statics, seam, tz, fx, fy, tx, ty, fseam, tiles):
    for tile in range(4):
        if tile not in tiles and tile + 1 not in tiles:
            continue
        east = table[1, at(tile), :]
        east_m, east_1 = lane_roll(east, 1), lane_roll(east, -1)
        north, north_m, north_1 = (table[2, at(tile, n), :] for n in (0, -1, 1))
        for k in range(K):
            for dom in doms:
                here, grad = x[dom, k, at(tile), :], tz[dom, k, at(tile), :]
                if tile in tiles:
                    right, left = lane_roll(here, -1), lane_roll(here, 1)
                    far = lane_roll(here, -2)
                    grad_right = lane_roll(grad, -1)
                    jump = jnp.where(east > k, right - here, 0.0)
                    before = jnp.where(east_m > k, here - left, 0.0)
                    after = jnp.where(east_1 > k, far - right, 0.0)
                    fx[dom, k, plain(tile), :] = face_flux(
                        *(statics[i, k, plain(tile), :] for i in range(4)),
                        here, right, before, jump, after, grad + grad_right,
                    )
                    tx[dom, k, plain(tile), :] = before + jump
                up, down, far = (x[dom, k, at(tile, n), :] for n in (1, -1, 2))
                grads = grad + tz[dom, k, at(tile, 1), :]
                jump = jnp.where(north > k, up - here, 0.0)
                before = jnp.where(north_m > k, here - down, 0.0)
                after = jnp.where(north_1 > k, far - up, 0.0)
                fy[dom, k, at(tile), :] = face_flux(
                    *(statics[i, k, plain(tile), :] for i in range(4, 8)),
                    here, up, before, jump, after, grads,
                )
                ty[dom, k, plain(tile), :] = before + jump
                if tile == 2 and 3 in tiles:
                    fseam[dom, k] = face_flux(
                        *(seam[i, k] for i in range(4)), here, up, before, jump, after, grads
                    )


def sum_pass(x, later, doms, table, statics, dz, fx, fy, tx, ty, fseam, tiles):
    first_row = lax.broadcasted_iota(jnp.int32, (8, LANES), 0) == 0
    for tile in tiles:
        rows = plain(tile)
        level = table[0, at(tile), :]
        for dom in doms:
            flux_above = None
            here, d_above = x[dom, 0, at(tile), :], None
            tx_here, ty_here = tx[dom, 0, rows, :], ty[dom, 0, rows, :]
            for k in range(K):
                f = fx[dom, k, rows, :]
                total = lane_roll(f, 1) - f
                south = fy[dom, k, at(tile, -1), :]
                if tile == 3:
                    south = jnp.where(first_row, row_roll(fseam[dom, k], 1), south)
                total = total + (south - fy[dom, k, at(tile), :])
                if flux_above is not None:
                    total = total + flux_above
                if k < K - 1:
                    below = x[dom, k + 1, at(tile), :]
                    tx_below, ty_below = tx[dom, k + 1, rows, :], ty[dom, k + 1, rows, :]
                    d = dz[dom, k, rows, :]
                    d_below = dz[dom, k + 1, rows, :] if k < K - 2 else jnp.zeros_like(d)
                    before = jnp.zeros_like(d) if d_above is None else d_above
                    c, h, g, a, b = (statics[i, k, rows, :] for i in range(8, 13))
                    down = c > 0
                    slope = minmod(jnp.where(down, before, d_below), d)
                    flux = c * (jnp.where(down, here, below) + h * slope) - (
                        g * d + a * (tx_here + tx_below) + b * (ty_here + ty_below)
                    )
                    total = total - flux
                    flux_above, d_above = flux, d
                later[dom, k, at(tile), :] = here + jnp.where(level > k, total, 0.0)
                if k < K - 1:
                    here, tx_here, ty_here = below, tx_below, ty_below


def unpack_south(band, raw, x, lev):
    for k in range(K):
        for f in range(STATICS):
            raw[f, k, 4:8, :] = band[k, 4 * f : 4 * f + 4, :]
        for n, f in enumerate(NORTHWARD):
            raw[f, k, 3:4, :] = band[k, 52 + n : 53 + n, :]
        for t in range(2):
            x[t, k, 10:16, :] = band[k, 40 + 6 * t : 46 + 6 * t, :]
        if k < 6:
            lev[2 + k : 3 + k, :] = band[k, 55:56, :]


def unpack_north(band, raw, x, lev, seam):
    for k in range(K):
        for f in range(STATICS):
            raw[f, k, 24:28, :] = band[k, 4 * f : 4 * f + 4, :]
        for t in range(2):
            x[t, k, 32:38, :] = band[k, 40 + 6 * t : 46 + 6 * t, :]
        if k < 6:
            lev[24 + k : 25 + k, :] = band[k, 55:56, :]
        for n, f in enumerate(NORTHWARD):
            seam[n, k] = raw[f, k, 16:24, :]


def unpack_fold(band, flat, raw, x, lev, seam):
    mirror = LANES - 1 - lanes_of((8, LANES))
    for k in range(K):
        for g in range(7):
            rows = slice(8 * g, 8 * g + 8)
            flat[k, rows, :] = jnp.take_along_axis(band[k, rows, :], mirror, axis=1)
        for f in range(STATICS):
            sign = -1.0 if f in FLIPPED else 1.0
            if f in NORTHWARD:
                n = f - NORTHWARD[0]
                seam[n, k, 7:8, :] = sign * flat[k, 4 * f + 3 : 4 * f + 4, :]
                order = [4 * f + 2, 4 * f + 1, 4 * f, 52 + n]
            else:
                order = [4 * f + 3, 4 * f + 2, 4 * f + 1, 4 * f]
            for r, source in enumerate(order):
                raw[f, k, 24 + r : 25 + r, :] = sign * flat[k, source : source + 1, :]
        for t in range(2):
            for r in range(6):
                source = 45 + 6 * t - r
                x[t, k, 32 + r : 33 + r, :] = flat[k, source : source + 1, :]
        if k < 6:
            lev[29 - k : 30 - k, :] = flat[k, 55:56, :]


def step_kernel(tracers, levels, *refs):
    statics = refs[:STATICS]
    near, far, merged, near_corner, far_corner, out = refs[STATICS : STATICS + 6]
    (raw, flat, x, xb, lev, seam, derived, seam_derived,
     halo, sraw, slev, sseam, sderived, sseam_derived,
     table, stable, dz, tz, fx, fy, tx, ty, fseam) = refs[STATICS + 6 :]
    even, top = is_even("lat"), is_top()
    lane8 = lanes_of((8, LANES))

    for f in range(STATICS):
        for k in range(K):
            raw[f, k, 8:24, :] = statics[f][k]
    for t in range(2):
        for k in range(K):
            x[t, k, 16:32, :] = tracers[t, k]
    lev[8:24, :] = levels[...].astype(jnp.float32)
    for tile in range(2):
        for v in range(SLOTS):
            halo[1 + tile, v] = merged[tile, v]

    @pl.when(even)
    def _():
        unpack_south(far, raw, x, lev)
        unpack_north(near, raw, x, lev, seam)
        for v in range(SLOTS):
            halo[0, v] = far_corner[v]
            halo[3, v] = near_corner[v]

    @pl.when(jnp.logical_not(even))
    def _():
        unpack_south(near, raw, x, lev)
        for v in range(SLOTS):
            halo[0, v] = near_corner[v]

        @pl.when(top)
        def _():
            unpack_fold(far, flat, raw, x, lev, seam)
            flip = (lane8 // 16) * 16 + 15 - lane8 % 16
            for v in range(SLOTS):
                turned = jnp.take_along_axis(far_corner[v], flip, axis=1)
                for r in range(8):
                    halo[3, v, r : r + 1, :] = turned[7 - r : 8 - r, :]

        @pl.when(jnp.logical_not(top))
        def _():
            unpack_north(far, raw, x, lev, seam)
            for v in range(SLOTS):
                halo[3, v] = far_corner[v]

    half = lane8 % 64
    in_halo = (half >= 24) & (half < 40)
    low, first = half < 24, lane8 < 64

    def strip(own, packed, slot):
        both = jnp.where(low, lane_roll(own, 24), lane_roll(own, 40))
        return jnp.where(in_halo, lane_roll(packed, 24 - 16 * (slot % 8)), both)

    def twice(strip64):
        return jnp.where(first, strip64, lane_roll(strip64, 64))

    for tile in range(4):
        rows = plain(tile)
        for f in range(STATICS):
            for k in range(K):
                slot = f * K + k
                sraw[f, k, rows, :] = strip(raw[f, k, rows, :], halo[tile, slot // 8], slot)
        for k in range(K):
            x[2, k, at(tile), :] = strip(x[0, k, at(tile), :], halo[tile, (120 + k) // 8], 120 + k)
            tz[0, k, at(tile), :] = strip(x[1, k, at(tile), :], halo[tile, (132 + k) // 8], 132 + k)
        slev[rows, :] = twice(strip(lev[rows, :], halo[tile, 18], 144))
    for tile in range(4):
        rows = plain(tile)
        for f in range(STATICS):
            for k in range(K):
                sraw[f, k, rows, :] = twice(sraw[f, k, rows, :])
        for k in range(K):
            x[2, k, at(tile), :] = jnp.where(
                first, x[2, k, at(tile), :], lane_roll(tz[0, k, at(tile), :], 64)
            )
    for n, f in enumerate(NORTHWARD):
        for k in range(K):
            sseam[n, k] = sraw[f, k, 16:24, :]

    @pl.when(top)
    def _():
        for f in range(STATICS):
            for k in range(K):
                slot = f * K + k
                v = sraw[f, k, 24:32, :]
                if f in FLIPPED:
                    v = jnp.where(in_halo, -v, v)
                if f in NORTHWARD:
                    n = f - NORTHWARD[0]
                    own = strip(seam[n, k], halo[3, slot // 8], slot)
                    sign = -1.0 if f in FLIPPED else 1.0
                    packed = lane_roll(halo[3, slot // 8], 24 - 16 * (slot % 8))
                    last = jnp.where(in_halo[:1], sign * packed[:1], own[7:8])
                    sseam[n, k, 7:8, :] = twice(jnp.concatenate([last] * 8, axis=0))[:1]
                    moved = row_roll(v, -1)
                    v = jnp.where(in_halo, moved, v)
                if f in EASTWARD:
                    v = lane_roll(v, -1)
                    raw[f, k, 24:32, :] = lane_roll(raw[f, k, 24:32, :], -1)
                sraw[f, k, 24:32, :] = v

    level_tables(lev[...], table)
    level_tables(slev[...], stable)
    derive(raw, derived, seam, seam_derived, table)
    derive(sraw, sderived, sseam, sseam_derived, stable)

    now, later = x, xb
    for step in range(STEPS):
        tiles = (1, 2) if step == STEPS - 1 else (0, 1, 2, 3)
        for doms, tab, der, sea in (
            ((0, 1), table, derived, seam_derived),
            ((2,), stable, sderived, sseam_derived),
        ):
            grads_pass(now, doms, tab, dz, tz)
            sides_pass(now, doms, tab, der, sea, tz, fx, fy, tx, ty, fseam, tiles)
            sum_pass(now, later, doms, tab, der, dz, fx, fy, tx, ty, fseam, tiles)
        now, later = later, now

    lane = lanes_of((8, LANES))
    for t in range(2):
        for k in range(K):
            for tile in (1, 2):
                s = now[2, k, at(tile), :]
                west, east = lane_roll(s, -40 - 64 * t), lane_roll(s, 104 - 64 * t)
                mid = now[t, k, at(tile), :]
                out[t, k, plain(tile - 1), :] = jnp.where(
                    lane < 6, west, jnp.where(lane >= 122, east, mid)
                )


def swaps(count, first, wrap):
    pairs = []
    for low in range(first, count if wrap else count - 1, 2):
        high = (low + 1) % count
        pairs += [(low, high), (high, low)]
    return pairs


def swap_lon(array):
    count = lax.axis_size("lon")
    return (
        lax.ppermute(array, "lon", swaps(count, 0, False)),
        lax.ppermute(array, "lon", swaps(count, 1, True)),
    )


def swap_lat(near, far):
    bands, count = lax.axis_size("lat"), lax.axis_size("lon")
    pairs = [
        (low * count + i, high * count + i)
        for low, high in swaps(bands, 1, False)
        for i in range(count)
    ]
    last = (bands - 1) * count
    pairs += [(last + i, last + count - 1 - i) for i in range(count)]
    return (
        lax.ppermute(near, "lat", swaps(bands, 0, False)),
        lax.ppermute(far, ("lat", "lon"), pairs),
    )


def shape(*dims):
    return jax.ShapeDtypeStruct(dims, jnp.float32)


def params(limit=VMEM_LIMIT):
    return pltpu.CompilerParams(vmem_limit_bytes=limit)


def body(tracers, wet_levels, ce, cn, cd, de, se, dn, sn, dd, dse, dsn):
    statics = (ce, de, se, cn, dn, sn, cd, dd, dse, dsn)
    sides = pl.pallas_call(
        side_kernel,
        out_shape=shape(2, SLOTS, 8, LANES),
        compiler_params=params(FULL),
        name="sides",
    )(tracers, wet_levels, *statics)
    near_side, far_side = swap_lon(sides)
    in_vmem = pl.BlockSpec(memory_space=pltpu.VMEM)
    near, far = pl.pallas_call(
        band_kernel,
        out_shape=(shape(K, 56, LANES), shape(K, 56, LANES)),
        in_specs=[in_vmem] * (2 + STATICS) + [pl.BlockSpec(memory_space=pl.ANY)],
        compiler_params=params(FULL),
        name="bands",
    )(tracers, wet_levels, *statics, far_side)
    near, far = swap_lat(near, far)
    merged, near_corner, far_corner = pl.pallas_call(
        corner_kernel,
        out_shape=(shape(2, SLOTS, 8, LANES), shape(SLOTS, 8, LANES), shape(SLOTS, 8, LANES)),
        compiler_params=params(),
        name="corners",
    )(near_side, far_side)
    near_corner, far_corner = swap_lat(near_corner, far_corner)
    return pl.pallas_call(
        step_kernel,
        out_shape=shape(2, K, ROWS, LANES),
        scratch_shapes=[
            pltpu.VMEM(dims, jnp.float32)
            for dims in (
                (STATICS, K, EXT, LANES),
                (K, 56, LANES),
                (3, K, PAD, LANES),
                (3, K, PAD, LANES),
                (EXT, LANES),
                (3, K, 8, LANES),
                (13, K, EXT, LANES),
                (4, K, 8, LANES),
                (4, SLOTS, 8, LANES),
                (STATICS, K, EXT, LANES),
                (EXT, LANES),
                (3, K, 8, LANES),
                (13, K, EXT, LANES),
                (4, K, 8, LANES),
                (3, PAD, LANES),
                (3, PAD, LANES),
                (3, K, EXT, LANES),
                (3, K, PAD, LANES),
                (3, K, EXT, LANES),
                (3, K, PAD, LANES),
                (3, K, EXT, LANES),
                (3, K, EXT, LANES),
                (3, K, 8, LANES),
            )
        ],
        compiler_params=params(),
        name="steps",
    )(tracers, wet_levels, *statics, near, far, merged, near_corner, far_corner)


def solution(mesh):
    field = P(None, "lat", "lon")
    whole = P(None, None, "lat", "lon")
    in_specs = (whole, P("lat", "lon")) + (field,) * STATICS
    return jax.shard_map(body, mesh=mesh, in_specs=in_specs, out_specs=whole, check_vma=False)
```

```python
import jax
import jax.numpy as jnp
from jax import lax
from jax.experimental import pallas as pl
from jax.experimental.pallas import tpu as pltpu
from jax.sharding import PartitionSpec as P

STEPS = 3
K = 12
ROWS = 16
LANES = 128
EXT = 32
PAD = 48
NORTHWARD = (3, 4, 5)
EASTWARD = (0, 1, 2)
FLIPPED = (0, 2, 3, 5, 8, 9)
STATICS = 10
SLOTS = 19
HALVES = 10
BAND = 56
VMEM_LIMIT = 48 * 1024 * 1024
FULL = 63 * 1024 * 1024


def lane_roll(x, shift):
    return pltpu.roll(x, shift % x.shape[-1], x.ndim - 1)


def row_roll(x, shift):
    return pltpu.roll(x, shift % x.shape[0], 0)


def lanes_of(shape):
    return lax.broadcasted_iota(jnp.int32, shape, len(shape) - 1)


def is_even(axis):
    return lax.rem(lax.axis_index(axis), 2) == 0


def is_top():
    return lax.axis_index("lat") == lax.axis_size("lat") - 1


def at_band(k, row, count):
    return slice(BAND * k + row, BAND * k + row + count)


def pack_band(dst, tracers, levels, statics, northward):
    low4 = ROWS - 4 if northward else 0
    low6 = ROWS - 6 if northward else 0
    extra = ROWS - 5 if northward else 0
    for k in range(K):
        for f in range(STATICS):
            dst[at_band(k, 4 * f, 4), :] = statics[f][k, low4 : low4 + 4, :]
        for t in range(2):
            dst[at_band(k, 40 + 6 * t, 6), :] = tracers[t, k, low6 : low6 + 6, :]
        for n, f in enumerate(NORTHWARD):
            dst[at_band(k, 52 + n, 1), :] = statics[f][k, extra : extra + 1, :]
        row = low6 + k if k < 6 else 0
        dst[at_band(k, 55, 1), :] = levels[row : row + 1, :].astype(jnp.float32)


def pack_kernel(tracers, levels, *refs):
    statics = refs[:STATICS]
    near, far, near_own, far_own, packed_all = refs[STATICS:]
    even = is_even("lat")

    @pl.when(even)
    def _():
        pack_band(near, tracers, levels, statics, True)
        pack_band(far, tracers, levels, statics, False)

    @pl.when(jnp.logical_not(even))
    def _():
        pack_band(far, tracers, levels, statics, True)
        pack_band(near, tracers, levels, statics, False)

    pack_sides(
        (1, 2), statics, tracers, None, None,
        lambda tile: levels[plain(tile - 1), :].astype(jnp.float32), near_own, far_own, packed_all,
    )


def pack_sides(tiles, statics, tracers, raw, x, level_of, near_side, far_side, packed_all):
    even_lon = is_even("lon")
    place = lanes_of((8, LANES)) // 16
    low = lanes_of((8, LANES)) % 16 < 8
    for at_tile, tile in enumerate(tiles):
        for v in range(SLOTS):
            packed = jnp.zeros((8, LANES), jnp.float32)
            for q in range(8):
                slot = 8 * v + q
                f, k = slot // K, slot % K
                if slot > 12 * K:
                    continue
                if slot == 12 * K:
                    value = level_of(tile)
                elif f < STATICS:
                    value = tile_of(statics, raw, (f, k), tile)
                else:
                    value = tile_of(tracers, x, (f - STATICS, k), tile)
                packed = jnp.where(place == q, lane_roll(value, 8 + 16 * q), packed)
            packed_all[at_tile, v] = packed
        packed_all[at_tile, SLOTS] = jnp.zeros((8, LANES), jnp.float32)
        for u in range(HALVES):
            one, two = packed_all[at_tile, 2 * u], packed_all[at_tile, 2 * u + 1]
            eastern = jnp.where(low, one, lane_roll(two, 8))
            western = jnp.where(low, lane_roll(one, -8), two)
            near_side[at_tile, u] = jnp.where(even_lon, eastern, western)
            far_side[at_tile, u] = jnp.where(even_lon, western, eastern)


def expand(halo, tile, u, near, far, western_near):
    low = lanes_of((8, LANES)) % 16 < 8
    western = jnp.where(western_near, near, far)
    eastern = jnp.where(western_near, far, near)
    halo[tile, 2 * u] = jnp.where(low, western, lane_roll(eastern, 8))
    halo[tile, 2 * u + 1] = jnp.where(low, lane_roll(western, -8), eastern)


def minmod(p, q):
    return jnp.maximum(jnp.minimum(p, q), 0.0) + jnp.minimum(jnp.maximum(p, q), 0.0)


def signed_half(c):
    return jnp.where(c > 0, 0.5, -0.5) - 0.5 * c


def face_flux(c, h, spread, tilt, here, there, before, jump, after, grads):
    up = c > 0
    slope = minmod(jnp.where(up, before, after), jump)
    return c * (jnp.where(up, here, there) + h * slope) - spread * (jump + tilt * grads)


def at(tile, shift=0):
    return slice(8 + 8 * tile + shift, 16 + 8 * tile + shift)


def plain(tile):
    return slice(8 * tile, 8 * tile + 8)


def level_tables(level, table):
    table[0, 8 : 8 + EXT, :] = level
    table[1, 8 : 8 + EXT, :] = jnp.minimum(level, lane_roll(level, -1))
    table[2, 8 : 8 + EXT, :] = jnp.minimum(level, row_roll(level, -1))


def derive(raw, put, seam_put, table):
    for tile in range(4):
        rows = plain(tile)
        level, east_level, north_level = (table[i, at(tile), :] for i in range(3))
        for k in range(K):
            east, north, lower = east_level > k, north_level > k, level > k + 1
            c = raw[0, k, rows, :]
            put[0, k, rows, :] = jnp.where(east, c, 0.0)
            put[1, k, rows, :] = signed_half(c)
            put[2, k, rows, :] = raw[1, k, rows, :]
            put[3, k, rows, :] = jnp.where(east, 0.25 * raw[2, k, rows, :], 0.0)
            c = raw[3, k, rows, :]
            put[4, k, rows, :] = jnp.where(north, c, 0.0)
            put[5, k, rows, :] = signed_half(c)
            put[6, k, rows, :] = raw[4, k, rows, :]
            put[7, k, rows, :] = jnp.where(north, 0.25 * raw[5, k, rows, :], 0.0)
            if tile == 2:
                c = raw[3, k, 24:32, :]
                seam_put[0, k] = jnp.where(north, c, 0.0)
                seam_put[1, k] = signed_half(c)
                seam_put[2, k] = raw[4, k, 24:32, :]
                seam_put[3, k] = jnp.where(north, 0.25 * raw[5, k, 24:32, :], 0.0)
            if k < K - 1:
                c, spread = raw[6, k, rows, :], raw[7, k, rows, :]
                along, across = raw[8, k, rows, :], raw[9, k, rows, :]
                put[8, k, rows, :] = jnp.where(lower, c, 0.0)
                put[9, k, rows, :] = signed_half(c)
                put[10, k, rows, :] = spread * (along * along + across * across)
                masked = jnp.where(lower, 0.25 * spread, 0.0)
                put[11, k, rows, :] = masked * along
                put[12, k, rows, :] = masked * across


def grads_pass(x, doms, table, dz, tz):
    for tile in range(4):
        level = table[0, at(tile), :]
        for dom in doms:
            above = None
            here = x[dom, 0, at(tile), :]
            for k in range(K):
                if k < K - 1:
                    below = x[dom, k + 1, at(tile), :]
                    d = jnp.where(level > k + 1, below - here, 0.0)
                    dz[dom, k, plain(tile), :] = d
                    tz[dom, k, at(tile), :] = d if above is None else above + d
                    here, above = below, d
                else:
                    tz[dom, k, at(tile), :] = above


def sides_pass(x, doms, table, statics, seam, tz, fx, fy, tx, ty, fseam, tiles):
    for tile in range(4):
        if tile not in tiles and tile + 1 not in tiles:
            continue
        east = table[1, at(tile), :]
        east_m, east_1 = lane_roll(east, 1), lane_roll(east, -1)
        north, north_m, north_1 = (table[2, at(tile, n), :] for n in (0, -1, 1))
        for k in range(K):
            for dom in doms:
                here, grad = x[dom, k, at(tile), :], tz[dom, k, at(tile), :]
                if tile in tiles:
                    right, left = lane_roll(here, -1), lane_roll(here, 1)
                    far = lane_roll(here, -2)
                    grad_right = lane_roll(grad, -1)
                    jump = jnp.where(east > k, right - here, 0.0)
                    before = jnp.where(east_m > k, here - left, 0.0)
                    after = jnp.where(east_1 > k, far - right, 0.0)
                    fx[dom, k, plain(tile), :] = face_flux(
                        *(statics[i, k, plain(tile), :] for i in range(4)),
                        here, right, before, jump, after, grad + grad_right,
                    )
                    tx[dom, k, plain(tile), :] = before + jump
                up, down, far = (x[dom, k, at(tile, n), :] for n in (1, -1, 2))
                grads = grad + tz[dom, k, at(tile, 1), :]
                jump = jnp.where(north > k, up - here, 0.0)
                before = jnp.where(north_m > k, here - down, 0.0)
                after = jnp.where(north_1 > k, far - up, 0.0)
                fy[dom, k, at(tile), :] = face_flux(
                    *(statics[i, k, plain(tile), :] for i in range(4, 8)),
                    here, up, before, jump, after, grads,
                )
                ty[dom, k, plain(tile), :] = before + jump
                if tile == 2 and 3 in tiles:
                    fseam[dom, k] = face_flux(
                        *(seam[i, k] for i in range(4)), here, up, before, jump, after, grads
                    )


def sum_pass(x, later, doms, table, statics, dz, fx, fy, tx, ty, fseam, tiles):
    first_row = lax.broadcasted_iota(jnp.int32, (8, LANES), 0) == 0
    for tile in tiles:
        rows = plain(tile)
        level = table[0, at(tile), :]
        for dom in doms:
            flux_above = None
            here, d_above = x[dom, 0, at(tile), :], None
            tx_here, ty_here = tx[dom, 0, rows, :], ty[dom, 0, rows, :]
            for k in range(K):
                f = fx[dom, k, rows, :]
                total = lane_roll(f, 1) - f
                south = fy[dom, k, at(tile, -1), :]
                if tile == 3:
                    south = jnp.where(first_row, row_roll(fseam[dom, k], 1), south)
                total = total + (south - fy[dom, k, at(tile), :])
                if flux_above is not None:
                    total = total + flux_above
                if k < K - 1:
                    below = x[dom, k + 1, at(tile), :]
                    tx_below, ty_below = tx[dom, k + 1, rows, :], ty[dom, k + 1, rows, :]
                    d = dz[dom, k, rows, :]
                    d_below = dz[dom, k + 1, rows, :] if k < K - 2 else jnp.zeros_like(d)
                    before = jnp.zeros_like(d) if d_above is None else d_above
                    c, h, g, a, b = (statics[i, k, rows, :] for i in range(8, 13))
                    down = c > 0
                    slope = minmod(jnp.where(down, before, d_below), d)
                    flux = c * (jnp.where(down, here, below) + h * slope) - (
                        g * d + a * (tx_here + tx_below) + b * (ty_here + ty_below)
                    )
                    total = total - flux
                    flux_above, d_above = flux, d
                later[dom, k, at(tile), :] = here + jnp.where(level > k, total, 0.0)
                if k < K - 1:
                    here, tx_here, ty_here = below, tx_below, ty_below


def unpack_south(band, raw, x, lev):
    for k in range(K):
        for f in range(STATICS):
            raw[f, k, 4:8, :] = band[at_band(k, 4 * f, 4), :]
        for n, f in enumerate(NORTHWARD):
            raw[f, k, 3:4, :] = band[at_band(k, 52 + n, 1), :]
        for t in range(2):
            x[t, k, 2:8, :] = band[at_band(k, 40 + 6 * t, 6), :]
        if k < 6:
            lev[2 + k : 3 + k, :] = band[at_band(k, 55, 1), :]


def unpack_north(band, raw, x, lev):
    for k in range(K):
        for f in range(STATICS):
            raw[f, k, 8:12, :] = band[at_band(k, 4 * f, 4), :]
        for t in range(2):
            x[t, k, 8:14, :] = band[at_band(k, 40 + 6 * t, 6), :]
        if k < 6:
            lev[8 + k : 9 + k, :] = band[at_band(k, 55, 1), :]


def unpack_fold(band, flat, raw, x, lev):
    mirror = LANES - 1 - lanes_of((8, LANES))
    for k in range(K):
        for g in range(7):
            rows = slice(8 * g, 8 * g + 8)
            flat[k, rows, :] = jnp.take_along_axis(band[at_band(k, 8 * g, 8), :], mirror, axis=1)
        for f in range(STATICS):
            sign = -1.0 if f in FLIPPED else 1.0
            order = [4 * f + 3, 4 * f + 2, 4 * f + 1, 4 * f]
            if f in NORTHWARD:
                raw[f, k, 15:16, :] = sign * flat[k, order[0] : order[0] + 1, :]
                order = order[1:] + [52 + f - NORTHWARD[0]]
            for r, source in enumerate(order):
                raw[f, k, 8 + r : 9 + r, :] = sign * flat[k, source : source + 1, :]
        for t in range(2):
            for r in range(6):
                source = 45 + 6 * t - r
                x[t, k, 8 + r : 9 + r, :] = flat[k, source : source + 1, :]
        if k < 6:
            lev[13 - k : 14 - k, :] = flat[k, 55:56, :]


def middle_kernel(near, far, *refs):
    raw, x, lev, near_side, far_side, flat, packed_all = refs
    even, top = is_even("lat"), is_top()

    @pl.when(even)
    def _():
        unpack_south(far, raw, x, lev)
        unpack_north(near, raw, x, lev)

    @pl.when(jnp.logical_not(even))
    def _():
        unpack_south(near, raw, x, lev)

        @pl.when(top)
        def _():
            unpack_fold(far, flat, raw, x, lev)

        @pl.when(jnp.logical_not(top))
        def _():
            unpack_north(far, raw, x, lev)
    pack_sides(
        (0, 3), None, None, raw, x, lambda tile: lev[plain(tile // 3), :],
        near_side, far_side, packed_all,
    )


def tile_of(own, beside, where, tile):
    i, k = where
    if tile in (1, 2):
        return own[i][k, plain(tile - 1), :] if isinstance(own, tuple) else own[i, k, plain(tile - 1), :]
    return beside[i, k, plain(tile // 3), :]


def run_steps(x, xb, doms, raw, table, derived, seam_derived, work):
    dz, tz, fx, fy, tx, ty, fseam = work
    derive(raw, derived, seam_derived, table)
    now, later = x, xb
    for step in range(STEPS):
        tiles = (1, 2) if step == STEPS - 1 else (0, 1, 2, 3)
        grads_pass(now, doms, table, dz, tz)
        sides_pass(now, doms, table, derived, seam_derived, tz, fx, fy, tx, ty, fseam, tiles)
        sum_pass(now, later, doms, table, derived, dz, fx, fy, tx, ty, fseam, tiles)
        now, later = later, now
    return now


def level_of(levels, beside, tile):
    if tile in (1, 2):
        return levels[plain(tile - 1), :].astype(jnp.float32)
    return beside[plain(tile // 3), :]


def shift_fold(raw):
    @pl.when(jnp.logical_not(is_top()))
    def _():
        for f in NORTHWARD:
            for k in range(K):
                raw[f, k, 31:32, :] = raw[f, k, 23:24, :]

    @pl.when(is_top())
    def _():
        for f in EASTWARD:
            for k in range(K):
                raw[f, k, 24:32, :] = lane_roll(raw[f, k, 24:32, :], -1)


def main_kernel(tracers, levels, *refs):
    statics = refs[:STATICS]
    beside, x_beside, lev, out, raw, x, xb, table, derived, seam_derived = refs[STATICS : STATICS + 10]
    for tile in range(4):
        for k in range(K):
            for f in range(STATICS):
                raw[f, k, plain(tile), :] = tile_of(statics, beside, (f, k), tile)
            for t in range(2):
                x[t, k, at(tile), :] = tile_of(tracers, x_beside, (t, k), tile)
    shift_fold(raw)
    level = jnp.concatenate([level_of(levels, lev, tile) for tile in range(4)], axis=0)
    level_tables(level, table)
    now = run_steps(x, xb, (0, 1), raw, table, derived, seam_derived, refs[STATICS + 10 :])
    for t in range(2):
        for k in range(K):
            out[t, k] = now[t, k, 16:32, :]


def strip_kernel(tracers, levels, *refs):
    statics = refs[:STATICS]
    beside, x_beside, lev, near_own, far_own, near_side, far_side, middle, out = refs[STATICS : STATICS + 9]
    raw, x, xb, table, derived, seam_derived, halo, slev, second = refs[STATICS + 9 : STATICS + 18]
    even_lon = is_even("lon")
    for tile in range(4):
        for u in range(HALVES):
            a, b = (near_own, far_own) if tile in (1, 2) else (near_side, far_side)
            at_tile = (0, 0, 1, 1)[tile]
            expand(halo, tile, u, a[at_tile, u], b[at_tile, u], even_lon)

    lane8 = lanes_of((8, LANES))
    half = lane8 % 64
    in_halo = (half >= 24) & (half < 40)
    low, first = half < 24, lane8 < 64

    def strip(own, tile, slot):
        both = jnp.where(low, lane_roll(own, 24), lane_roll(own, 40))
        packed = halo[tile, slot // 8]
        return jnp.where(in_halo, lane_roll(packed, 24 - 16 * (slot % 8)), both)

    def twice(strip64):
        return jnp.where(first, strip64, lane_roll(strip64, 64))

    for tile in range(4):
        rows = plain(tile)
        for f in range(STATICS):
            for k in range(K):
                own = tile_of(statics, beside, (f, k), tile)
                raw[f, k, rows, :] = strip(own, tile, f * K + k)
        for k in range(K):
            own = [tile_of(tracers, x_beside, (t, k), tile) for t in range(2)]
            x[0, k, at(tile), :] = strip(own[0], tile, 120 + k)
            second[k, rows, :] = strip(own[1], tile, 132 + k)
        slev[rows, :] = twice(strip(level_of(levels, lev, tile), tile, 144))
    for tile in range(4):
        rows = plain(tile)
        for f in range(STATICS):
            for k in range(K):
                raw[f, k, rows, :] = twice(raw[f, k, rows, :])
        for k in range(K):
            x[0, k, at(tile), :] = jnp.where(
                first, x[0, k, at(tile), :], lane_roll(second[k, rows, :], 64)
            )
    shift_fold(raw)
    level_tables(slev[...], table)
    now = run_steps(x, xb, (0,), raw, table, derived, seam_derived, refs[STATICS + 18 :])
    for t in range(2):
        for k in range(K):
            for tile in (1, 2):
                s = now[0, k, at(tile), :]
                west, east = lane_roll(s, -40 - 64 * t), lane_roll(s, 104 - 64 * t)
                rows = plain(tile - 1)
                out[t, k, rows, :] = jnp.where(
                    lane8 < 6, west, jnp.where(lane8 >= 122, east, middle[t, k, rows, :])
                )


def swaps(count, first, wrap):
    pairs = []
    for low in range(first, count if wrap else count - 1, 2):
        high = (low + 1) % count
        pairs += [(low, high), (high, low)]
    return pairs


def swap(array, lat, lon):
    bands, count = lax.axis_size("lat"), lax.axis_size("lon")
    if lat is None:
        return lax.ppermute(array, "lon", swaps(count, lon, True))
    columns = list(range(count))
    if lon is not None:
        for low, high in swaps(count, lon, True):
            columns[low] = high
    pairs = [
        (low * count + i, high * count + columns[i])
        for low, high in swaps(bands, lat, False)
        for i in range(count)
    ]
    if lat == 1:
        last = (bands - 1) * count
        pairs += [(last + i, last + count - 1 - columns[i]) for i in range(count)]
    return lax.ppermute(array, ("lat", "lon"), pairs)


def shape(*dims):
    return jax.ShapeDtypeStruct(dims, jnp.float32)


def params(limit=VMEM_LIMIT):
    return pltpu.CompilerParams(vmem_limit_bytes=limit)


def body(tracers, wet_levels, ce, cn, cd, de, se, dn, sn, dd, dse, dsn):
    statics = (ce, de, se, cn, dn, sn, cd, dd, dse, dsn)
    band, side, own = shape(BAND * K, LANES), shape(2, HALVES, 8, LANES), shape(2, HALVES, 8, LANES)
    near, far, near_own, far_own = pl.pallas_call(
        pack_kernel,
        out_shape=(band, band, own, own),
        scratch_shapes=vmem((2, SLOTS + 1, 8, LANES)),
        compiler_params=params(FULL),
        name="pack",
    )(tracers, wet_levels, *statics)
    far = swap(far, 1, None)
    near = swap(near, 0, None)
    near_own = swap(near_own, None, 0)
    far_own = swap(far_own, None, 1)
    beside, x_beside, lev, near_side, far_side = pl.pallas_call(
        middle_kernel,
        out_shape=(
            shape(STATICS, K, 16, LANES), shape(2, K, 16, LANES), shape(16, LANES), side, side,
        ),
        scratch_shapes=vmem((K, BAND, LANES), (2, SLOTS + 1, 8, LANES)),
        compiler_params=params(),
        name="middle",
    )(near, far)
    far_side = swap(far_side, None, 1)
    near_side = swap(near_side, None, 0)
    inner = pl.pallas_call(
        main_kernel,
        out_shape=shape(2, K, ROWS, LANES),
        scratch_shapes=step_scratch(2),
        compiler_params=params(),
        cost_estimate=pl.CostEstimate(flops=20_000_000, bytes_accessed=20_000_000, transcendentals=0),
        name="blocks",
    )(tracers, wet_levels, *statics, beside, x_beside, lev)
    return pl.pallas_call(
        strip_kernel,
        out_shape=shape(2, K, ROWS, LANES),
        scratch_shapes=step_scratch(1, (4, SLOTS + 1, 8, LANES), (EXT, LANES), (K, EXT, LANES)),
        compiler_params=params(),
        name="strips",
    )(
        tracers, wet_levels, *statics, beside, x_beside, lev,
        near_own, far_own, near_side, far_side, inner,
    )


def vmem(*all_dims):
    return [pltpu.VMEM(dims, jnp.float32) for dims in all_dims]


def step_scratch(doms, *more):
    flat, padded = (doms, K, EXT, LANES), (doms, K, PAD, LANES)
    return vmem(
        (STATICS, K, EXT, LANES), padded, padded, (3, PAD, LANES),
        (13, K, EXT, LANES), (4, K, 8, LANES), *more,
        flat, padded, flat, padded, flat, flat, (doms, K, 8, LANES),
    )


def solution(mesh):
    field = P(None, "lat", "lon")
    whole = P(None, None, "lat", "lon")
    in_specs = (whole, P("lat", "lon")) + (field,) * STATICS
    return jax.shard_map(body, mesh=mesh, in_specs=in_specs, out_specs=whole, check_vma=False)
```

```python
import jax
import jax.numpy as jnp
from jax import lax
from jax.experimental import pallas as pl
from jax.experimental.pallas import tpu as pltpu
from jax.sharding import PartitionSpec as P

STEPS = 3
K = 12
ROWS = 16
LANES = 128
EXT = 32
PAD = 48
NORTHWARD = (3, 4, 5)
EASTWARD = (0, 1, 2)
FLIPPED = (0, 2, 3, 5, 8, 9)
STATICS = 10
SLOTS = 19
HALVES = 10
BAND = 56
VMEM_LIMIT = 48 * 1024 * 1024
FULL = 63 * 1024 * 1024


def lane_roll(x, shift):
    return pltpu.roll(x, shift % x.shape[-1], x.ndim - 1)


def row_roll(x, shift):
    return pltpu.roll(x, shift % x.shape[0], 0)


def lanes_of(shape):
    return lax.broadcasted_iota(jnp.int32, shape, len(shape) - 1)


def is_even(axis):
    return lax.rem(lax.axis_index(axis), 2) == 0


def is_top():
    return lax.axis_index("lat") == lax.axis_size("lat") - 1


def at_band(k, row, count):
    return slice(BAND * k + row, BAND * k + row + count)


def pack_band(dst, tracers, levels, statics, northward):
    low4 = ROWS - 4 if northward else 0
    low6 = ROWS - 6 if northward else 0
    extra = ROWS - 5 if northward else 0
    for k in range(K):
        for f in range(STATICS):
            dst[at_band(k, 4 * f, 4), :] = statics[f][k, low4 : low4 + 4, :]
        for t in range(2):
            dst[at_band(k, 40 + 6 * t, 6), :] = tracers[t, k, low6 : low6 + 6, :]
        for n, f in enumerate(NORTHWARD):
            dst[at_band(k, 52 + n, 1), :] = statics[f][k, extra : extra + 1, :]
        row = low6 + k if k < 6 else 0
        dst[at_band(k, 55, 1), :] = levels[row : row + 1, :].astype(jnp.float32)


def pack_kernel(tracers, levels, *refs):
    statics = refs[:STATICS]
    near, far, near_own, far_own, packed_all = refs[STATICS:]
    even = is_even("lat")

    @pl.when(even)
    def _():
        pack_band(near, tracers, levels, statics, True)
        pack_band(far, tracers, levels, statics, False)

    @pl.when(jnp.logical_not(even))
    def _():
        pack_band(far, tracers, levels, statics, True)
        pack_band(near, tracers, levels, statics, False)

    pack_sides(
        (1, 2), statics, tracers, None, None,
        lambda tile: levels[plain(tile - 1), :].astype(jnp.float32), near_own, far_own, packed_all,
    )


def pack_sides(tiles, statics, tracers, raw, x, level_of, near_side, far_side, packed_all):
    even_lon = is_even("lon")
    place = lanes_of((8, LANES)) // 16
    low = lanes_of((8, LANES)) % 16 < 8
    for at_tile, tile in enumerate(tiles):
        for v in range(SLOTS):
            packed = jnp.zeros((8, LANES), jnp.float32)
            for q in range(8):
                slot = 8 * v + q
                f, k = slot // K, slot % K
                if slot > 12 * K:
                    continue
                if slot == 12 * K:
                    value = level_of(tile)
                elif f < STATICS:
                    value = tile_of(statics, raw, (f, k), tile)
                else:
                    value = tile_of(tracers, x, (f - STATICS, k), tile)
                packed = jnp.where(place == q, lane_roll(value, 8 + 16 * q), packed)
            packed_all[at_tile, v] = packed
        packed_all[at_tile, SLOTS] = jnp.zeros((8, LANES), jnp.float32)
        for u in range(HALVES):
            one, two = packed_all[at_tile, 2 * u], packed_all[at_tile, 2 * u + 1]
            eastern = jnp.where(low, one, lane_roll(two, 8))
            western = jnp.where(low, lane_roll(one, -8), two)
            near_side[at_tile, u] = jnp.where(even_lon, eastern, western)
            far_side[at_tile, u] = jnp.where(even_lon, western, eastern)


def expand(halo, tile, u, near, far, western_near):
    low = lanes_of((8, LANES)) % 16 < 8
    western = jnp.where(western_near, near, far)
    eastern = jnp.where(western_near, far, near)
    halo[tile, 2 * u] = jnp.where(low, western, lane_roll(eastern, 8))
    halo[tile, 2 * u + 1] = jnp.where(low, lane_roll(western, -8), eastern)


def minmod(p, q):
    return jnp.maximum(jnp.minimum(p, q), 0.0) + jnp.minimum(jnp.maximum(p, q), 0.0)


def signed_half(c):
    return jnp.where(c > 0, 0.5, -0.5) - 0.5 * c


def face_flux(c, h, spread, tilt, here, there, before, jump, after, grads):
    up = c > 0
    slope = minmod(jnp.where(up, before, after), jump)
    return c * (jnp.where(up, here, there) + h * slope) - spread * (jump + tilt * grads)


def at(tile, shift=0):
    return slice(8 + 8 * tile + shift, 16 + 8 * tile + shift)


def plain(tile):
    return slice(8 * tile, 8 * tile + 8)


def level_tables(level, table):
    table[0, 8 : 8 + EXT, :] = level
    table[1, 8 : 8 + EXT, :] = jnp.minimum(level, lane_roll(level, -1))
    table[2, 8 : 8 + EXT, :] = jnp.minimum(level, row_roll(level, -1))


def derive(raw, put, seam_put, table):
    for tile in range(4):
        rows = plain(tile)
        level, east_level, north_level = (table[i, at(tile), :] for i in range(3))
        for k in range(K):
            east, north, lower = east_level > k, north_level > k, level > k + 1
            c = raw[0, k, rows, :]
            put[0, k, rows, :] = jnp.where(east, c, 0.0)
            put[1, k, rows, :] = signed_half(c)
            put[2, k, rows, :] = raw[1, k, rows, :]
            put[3, k, rows, :] = jnp.where(east, 0.25 * raw[2, k, rows, :], 0.0)
            c = raw[3, k, rows, :]
            put[4, k, rows, :] = jnp.where(north, c, 0.0)
            put[5, k, rows, :] = signed_half(c)
            put[6, k, rows, :] = raw[4, k, rows, :]
            put[7, k, rows, :] = jnp.where(north, 0.25 * raw[5, k, rows, :], 0.0)
            if tile == 2:
                c = raw[3, k, 24:32, :]
                seam_put[0, k] = jnp.where(north, c, 0.0)
                seam_put[1, k] = signed_half(c)
                seam_put[2, k] = raw[4, k, 24:32, :]
                seam_put[3, k] = jnp.where(north, 0.25 * raw[5, k, 24:32, :], 0.0)
            if k < K - 1:
                c, spread = raw[6, k, rows, :], raw[7, k, rows, :]
                along, across = raw[8, k, rows, :], raw[9, k, rows, :]
                put[8, k, rows, :] = jnp.where(lower, c, 0.0)
                put[9, k, rows, :] = signed_half(c)
                put[10, k, rows, :] = spread * (along * along + across * across)
                masked = jnp.where(lower, 0.25 * spread, 0.0)
                put[11, k, rows, :] = masked * along
                put[12, k, rows, :] = masked * across


def grads_pass(x, doms, table, dz, tz):
    for tile in range(4):
        level = table[0, at(tile), :]
        for dom in doms:
            above = None
            here = x[dom, 0, at(tile), :]
            for k in range(K):
                if k < K - 1:
                    below = x[dom, k + 1, at(tile), :]
                    d = jnp.where(level > k + 1, below - here, 0.0)
                    dz[dom, k, plain(tile), :] = d
                    tz[dom, k, at(tile), :] = d if above is None else above + d
                    here, above = below, d
                else:
                    tz[dom, k, at(tile), :] = above


def sides_pass(x, doms, table, statics, seam, tz, fx, fy, tx, ty, fseam, tiles):
    for tile in range(4):
        if tile not in tiles and tile + 1 not in tiles:
            continue
        east = table[1, at(tile), :]
        east_m, east_1 = lane_roll(east, 1), lane_roll(east, -1)
        north, north_m, north_1 = (table[2, at(tile, n), :] for n in (0, -1, 1))
        for k in range(K):
            for dom in doms:
                here, grad = x[dom, k, at(tile), :], tz[dom, k, at(tile), :]
                if tile in tiles:
                    right, left = lane_roll(here, -1), lane_roll(here, 1)
                    far = lane_roll(here, -2)
                    grad_right = lane_roll(grad, -1)
                    jump = jnp.where(east > k, right - here, 0.0)
                    before = jnp.where(east_m > k, here - left, 0.0)
                    after = jnp.where(east_1 > k, far - right, 0.0)
                    fx[dom, k, plain(tile), :] = face_flux(
                        *(statics[i, k, plain(tile), :] for i in range(4)),
                        here, right, before, jump, after, grad + grad_right,
                    )
                    tx[dom, k, plain(tile), :] = before + jump
                up, down, far = (x[dom, k, at(tile, n), :] for n in (1, -1, 2))
                grads = grad + tz[dom, k, at(tile, 1), :]
                jump = jnp.where(north > k, up - here, 0.0)
                before = jnp.where(north_m > k, here - down, 0.0)
                after = jnp.where(north_1 > k, far - up, 0.0)
                fy[dom, k, at(tile), :] = face_flux(
                    *(statics[i, k, plain(tile), :] for i in range(4, 8)),
                    here, up, before, jump, after, grads,
                )
                ty[dom, k, plain(tile), :] = before + jump
                if tile == 2 and 3 in tiles:
                    fseam[dom, k] = face_flux(
                        *(seam[i, k] for i in range(4)), here, up, before, jump, after, grads
                    )


def sum_pass(x, later, doms, table, statics, dz, fx, fy, tx, ty, fseam, tiles):
    first_row = lax.broadcasted_iota(jnp.int32, (8, LANES), 0) == 0
    for tile in tiles:
        rows = plain(tile)
        level = table[0, at(tile), :]
        for dom in doms:
            flux_above = None
            here, d_above = x[dom, 0, at(tile), :], None
            tx_here, ty_here = tx[dom, 0, rows, :], ty[dom, 0, rows, :]
            for k in range(K):
                f = fx[dom, k, rows, :]
                total = lane_roll(f, 1) - f
                south = fy[dom, k, at(tile, -1), :]
                if tile == 3:
                    south = jnp.where(first_row, row_roll(fseam[dom, k], 1), south)
                total = total + (south - fy[dom, k, at(tile), :])
                if flux_above is not None:
                    total = total + flux_above
                if k < K - 1:
                    below = x[dom, k + 1, at(tile), :]
                    tx_below, ty_below = tx[dom, k + 1, rows, :], ty[dom, k + 1, rows, :]
                    d = dz[dom, k, rows, :]
                    d_below = dz[dom, k + 1, rows, :] if k < K - 2 else jnp.zeros_like(d)
                    before = jnp.zeros_like(d) if d_above is None else d_above
                    c, h, g, a, b = (statics[i, k, rows, :] for i in range(8, 13))
                    down = c > 0
                    slope = minmod(jnp.where(down, before, d_below), d)
                    flux = c * (jnp.where(down, here, below) + h * slope) - (
                        g * d + a * (tx_here + tx_below) + b * (ty_here + ty_below)
                    )
                    total = total - flux
                    flux_above, d_above = flux, d
                later[dom, k, at(tile), :] = here + jnp.where(level > k, total, 0.0)
                if k < K - 1:
                    here, tx_here, ty_here = below, tx_below, ty_below


def unpack_south(band, raw, x, lev):
    for k in range(K):
        for f in range(STATICS):
            raw[f, k, 4:8, :] = band[at_band(k, 4 * f, 4), :]
        for n, f in enumerate(NORTHWARD):
            raw[f, k, 3:4, :] = band[at_band(k, 52 + n, 1), :]
        for t in range(2):
            x[t, k, 2:8, :] = band[at_band(k, 40 + 6 * t, 6), :]
        if k < 6:
            lev[2 + k : 3 + k, :] = band[at_band(k, 55, 1), :]


def unpack_north(band, raw, x, lev):
    for k in range(K):
        for f in range(STATICS):
            raw[f, k, 8:12, :] = band[at_band(k, 4 * f, 4), :]
        for t in range(2):
            x[t, k, 8:14, :] = band[at_band(k, 40 + 6 * t, 6), :]
        if k < 6:
            lev[8 + k : 9 + k, :] = band[at_band(k, 55, 1), :]


def unpack_fold(band, flat, raw, x, lev):
    mirror = LANES - 1 - lanes_of((8, LANES))
    for k in range(K):
        for g in range(7):
            rows = slice(8 * g, 8 * g + 8)
            flat[k, rows, :] = jnp.take_along_axis(band[at_band(k, 8 * g, 8), :], mirror, axis=1)
        for f in range(STATICS):
            sign = -1.0 if f in FLIPPED else 1.0
            order = [4 * f + 3, 4 * f + 2, 4 * f + 1, 4 * f]
            if f in NORTHWARD:
                raw[f, k, 15:16, :] = sign * flat[k, order[0] : order[0] + 1, :]
                order = order[1:] + [52 + f - NORTHWARD[0]]
            for r, source in enumerate(order):
                raw[f, k, 8 + r : 9 + r, :] = sign * flat[k, source : source + 1, :]
        for t in range(2):
            for r in range(6):
                source = 45 + 6 * t - r
                x[t, k, 8 + r : 9 + r, :] = flat[k, source : source + 1, :]
        if k < 6:
            lev[13 - k : 14 - k, :] = flat[k, 55:56, :]


def middle_kernel(near, far, *refs):
    raw, x, lev, near_side, far_side, flat, packed_all = refs
    even, top = is_even("lat"), is_top()

    @pl.when(even)
    def _():
        unpack_south(far, raw, x, lev)
        unpack_north(near, raw, x, lev)

    @pl.when(jnp.logical_not(even))
    def _():
        unpack_south(near, raw, x, lev)

        @pl.when(top)
        def _():
            unpack_fold(far, flat, raw, x, lev)

        @pl.when(jnp.logical_not(top))
        def _():
            unpack_north(far, raw, x, lev)
    pack_sides(
        (0, 3), None, None, raw, x, lambda tile: lev[plain(tile // 3), :],
        near_side, far_side, packed_all,
    )


def tile_of(own, beside, where, tile):
    i, k = where
    if tile in (1, 2):
        return own[i][k, plain(tile - 1), :] if isinstance(own, tuple) else own[i, k, plain(tile - 1), :]
    return beside[i, k, plain(tile // 3), :]


def run_steps(x, xb, doms, raw, table, derived, seam_derived, work):
    dz, tz, fx, fy, tx, ty, fseam = work
    derive(raw, derived, seam_derived, table)
    now, later = x, xb
    for step in range(STEPS):
        tiles = (1, 2) if step == STEPS - 1 else (0, 1, 2, 3)
        grads_pass(now, doms, table, dz, tz)
        sides_pass(now, doms, table, derived, seam_derived, tz, fx, fy, tx, ty, fseam, tiles)
        sum_pass(now, later, doms, table, derived, dz, fx, fy, tx, ty, fseam, tiles)
        now, later = later, now
    return now


def level_of(levels, beside, tile):
    if tile in (1, 2):
        return levels[plain(tile - 1), :].astype(jnp.float32)
    return beside[plain(tile // 3), :]


def shift_fold(raw):
    @pl.when(jnp.logical_not(is_top()))
    def _():
        for f in NORTHWARD:
            for k in range(K):
                raw[f, k, 31:32, :] = raw[f, k, 23:24, :]

    @pl.when(is_top())
    def _():
        for f in EASTWARD:
            for k in range(K):
                raw[f, k, 24:32, :] = lane_roll(raw[f, k, 24:32, :], -1)


def main_kernel(tracers, levels, *refs):
    statics = refs[:STATICS]
    beside, x_beside, lev, out, raw, x, xb, table, derived, seam_derived = refs[STATICS : STATICS + 10]
    for tile in range(4):
        for k in range(K):
            for f in range(STATICS):
                raw[f, k, plain(tile), :] = tile_of(statics, beside, (f, k), tile)
            for t in range(2):
                x[t, k, at(tile), :] = tile_of(tracers, x_beside, (t, k), tile)
    shift_fold(raw)
    level = jnp.concatenate([level_of(levels, lev, tile) for tile in range(4)], axis=0)
    level_tables(level, table)
    now = run_steps(x, xb, (0, 1), raw, table, derived, seam_derived, refs[STATICS + 10 :])
    for t in range(2):
        for k in range(K):
            out[t, k] = now[t, k, 16:32, :]


def strip_kernel(tracers, levels, *refs):
    statics = refs[:STATICS]
    beside, x_beside, lev, near_own, far_own, near_side, far_side, middle, out = refs[STATICS : STATICS + 9]
    raw, x, xb, table, derived, seam_derived, halo, slev, second = refs[STATICS + 9 : STATICS + 18]
    even_lon = is_even("lon")
    for tile in range(4):
        for u in range(HALVES):
            a, b = (near_own, far_own) if tile in (1, 2) else (near_side, far_side)
            at_tile = (0, 0, 1, 1)[tile]
            expand(halo, tile, u, a[at_tile, u], b[at_tile, u], even_lon)

    lane8 = lanes_of((8, LANES))
    in_halo, natural = lane8 < 16, lane8 >= 104
    first = natural | (lane8 < 40)

    def strip(own, tile, slot):
        both = jnp.where(natural, own, lane_roll(own, 16))
        packed = halo[tile, slot // 8]
        return jnp.where(in_halo, lane_roll(packed, -16 * (slot % 8)), both)

    def twice(strip64):
        return jnp.where(first, strip64, lane_roll(strip64, 64))

    for tile in range(4):
        rows = plain(tile)
        for f in range(STATICS):
            for k in range(K):
                own = tile_of(statics, beside, (f, k), tile)
                raw[f, k, rows, :] = strip(own, tile, f * K + k)
        for k in range(K):
            own = [tile_of(tracers, x_beside, (t, k), tile) for t in range(2)]
            x[0, k, at(tile), :] = strip(own[0], tile, 120 + k)
            second[k, rows, :] = strip(own[1], tile, 132 + k)
        slev[rows, :] = twice(strip(level_of(levels, lev, tile), tile, 144))
    for tile in range(4):
        rows = plain(tile)
        for f in range(STATICS):
            for k in range(K):
                raw[f, k, rows, :] = twice(raw[f, k, rows, :])
        for k in range(K):
            x[0, k, at(tile), :] = jnp.where(
                first, x[0, k, at(tile), :], lane_roll(second[k, rows, :], 64)
            )
    shift_fold(raw)
    level_tables(slev[...], table)
    now = run_steps(x, xb, (0,), raw, table, derived, seam_derived, refs[STATICS + 18 :])
    for t in range(2):
        for k in range(K):
            for tile in (1, 2):
                s = now[0, k, at(tile), :]
                west, east = lane_roll(s, -16 - 64 * t), lane_roll(s, 64) if t else s
                rows = plain(tile - 1)
                out[t, k, rows, :] = jnp.where(
                    lane8 < 6, west, jnp.where(lane8 >= 122, east, middle[t, k, rows, :])
                )


def swaps(count, first, wrap):
    pairs = []
    for low in range(first, count if wrap else count - 1, 2):
        high = (low + 1) % count
        pairs += [(low, high), (high, low)]
    return pairs


def swap(array, lat, lon):
    bands, count = lax.axis_size("lat"), lax.axis_size("lon")
    if lat is None:
        return lax.ppermute(array, "lon", swaps(count, lon, True))
    columns = list(range(count))
    if lon is not None:
        for low, high in swaps(count, lon, True):
            columns[low] = high
    pairs = [
        (low * count + i, high * count + columns[i])
        for low, high in swaps(bands, lat, False)
        for i in range(count)
    ]
    if lat == 1:
        last = (bands - 1) * count
        pairs += [(last + i, last + count - 1 - columns[i]) for i in range(count)]
    return lax.ppermute(array, ("lat", "lon"), pairs)


def shape(*dims):
    return jax.ShapeDtypeStruct(dims, jnp.float32)


def params(limit=VMEM_LIMIT):
    return pltpu.CompilerParams(vmem_limit_bytes=limit)


def body(tracers, wet_levels, ce, cn, cd, de, se, dn, sn, dd, dse, dsn):
    statics = (ce, de, se, cn, dn, sn, cd, dd, dse, dsn)
    band, side, own = shape(BAND * K, LANES), shape(2, HALVES, 8, LANES), shape(2, HALVES, 8, LANES)
    near, far, near_own, far_own = pl.pallas_call(
        pack_kernel,
        out_shape=(band, band, own, own),
        scratch_shapes=vmem((2, SLOTS + 1, 8, LANES)),
        compiler_params=params(FULL),
        name="pack",
    )(tracers, wet_levels, *statics)
    far = swap(far, 1, None)
    near = swap(near, 0, None)
    near_own = swap(near_own, None, 0)
    far_own = swap(far_own, None, 1)
    beside, x_beside, lev, near_side, far_side = pl.pallas_call(
        middle_kernel,
        out_shape=(
            shape(STATICS, K, 16, LANES), shape(2, K, 16, LANES), shape(16, LANES), side, side,
        ),
        scratch_shapes=vmem((K, BAND, LANES), (2, SLOTS + 1, 8, LANES)),
        compiler_params=params(),
        name="middle",
    )(near, far)
    far_side = swap(far_side, None, 1)
    near_side = swap(near_side, None, 0)
    inner = pl.pallas_call(
        main_kernel,
        out_shape=shape(2, K, ROWS, LANES),
        scratch_shapes=step_scratch(2),
        compiler_params=params(),
        cost_estimate=pl.CostEstimate(flops=20_000_000, bytes_accessed=20_000_000, transcendentals=0),
        name="blocks",
    )(tracers, wet_levels, *statics, beside, x_beside, lev)
    return pl.pallas_call(
        strip_kernel,
        out_shape=shape(2, K, ROWS, LANES),
        scratch_shapes=step_scratch(1, (4, SLOTS + 1, 8, LANES), (EXT, LANES), (K, EXT, LANES)),
        compiler_params=params(),
        name="strips",
    )(
        tracers, wet_levels, *statics, beside, x_beside, lev,
        near_own, far_own, near_side, far_side, inner,
    )


def vmem(*all_dims):
    return [pltpu.VMEM(dims, jnp.float32) for dims in all_dims]


def step_scratch(doms, *more):
    flat, padded = (doms, K, EXT, LANES), (doms, K, PAD, LANES)
    return vmem(
        (STATICS, K, EXT, LANES), padded, padded, (3, PAD, LANES),
        (13, K, EXT, LANES), (4, K, 8, LANES), *more,
        flat, padded, flat, padded, flat, flat, (doms, K, 8, LANES),
    )


def solution(mesh):
    field = P(None, "lat", "lon")
    whole = P(None, None, "lat", "lon")
    in_specs = (whole, P("lat", "lon")) + (field,) * STATICS
    return jax.shard_map(body, mesh=mesh, in_specs=in_specs, out_specs=whole, check_vma=False)
```
